512 devices in a mesh: outer: 128 (over z, y, core), inner: 4 (over x).
Axes of the slice: x: 4, y: 8, z: 8, core: 2. Of those that a mesh axis runs over, the one named last changes fastest.
Arguments:
- query_states: bfloat16 [65536, 4096], P(('outer', 'inner')), may hold values from -6 to 6
- key_states: bfloat16 [65536, 4096], P(('outer', 'inner')), may hold values from -6 to 6
- value_states: bfloat16 [65536, 4096], P(('outer', 'inner')), may hold values from -6 to 6
- doc_lengths: int32 [128], replicated, may hold values from 1 to 1024, 65536 in all
- slopes: float32 [32], replicated, may hold values from 0.00024414062 to 0.0625
Outputs:
- attended: bfloat16 [65536, 4096], P(('outer', 'inner'))
The draws below stay inside these ranges and needn't reach their ends.
Inputs may be any that keep to these rules, and one draw needn't show every extreme that they name: `doc_lengths`: the lengths add up to 65536; the longest is exactly 1024.
All inputs are finite; a program needn't handle non-finite values.
Results may differ from the reference program's by a relative error of at most 0.0045.
Values may be sent and summed in bfloat16 or wider, within the bound.
No kernel may reach another device: no remote copies, remote signals or barrier semaphores. Data moves between devices by JAX's collectives and lax.ppermute only.
A program may use at most 64 MiB of HBM per device.

```python
import math
import jax
import jax.numpy as jnp
import numpy as np
from jax import lax

H = 32
HD = 128
TOK_DEV = 128
TOKENS = 65536
DOC_MAX = 1024
DOCS = 128


def paired_draw(key):
    shape = (TOKENS, H * HD)
    query_key = jax.random.fold_in(key, 7001)
    second_key = jax.random.fold_in(key, 7002)
    row_ids = jnp.arange(TOKENS)[:, None]
    query_part = jnp.clip(jax.random.normal(query_key, shape, jnp.float32), -5.5, 5.5)
    key_part = jnp.clip(jax.random.normal(second_key, shape, jnp.float32), -5.5, 5.5)
    reach = DOC_MAX // 2
    far_signs = jax.random.rademacher(jax.random.fold_in(key, 7005), shape).astype(jnp.float32)
    far_vector = 5.5 * far_signs
    far_query = row_ids % 61 == 20
    query_part = jnp.where(far_query, far_vector, query_part)
    partner_row = row_ids + reach
    far_key = (partner_row % 61 == 20) & (partner_row < TOKENS)
    key_part = jnp.where(far_key, jnp.roll(far_vector, -reach, axis=0), key_part)
    return (query_part, key_part)


def draw_query_states(key, part):
    return paired_draw(key)[0].astype(jnp.bfloat16)


def draw_key_states(key, part):
    return paired_draw(key)[1].astype(jnp.bfloat16)


def draw_slopes(key, part):
    lowest = jnp.float32(0.25 / DOC_MAX)
    highest = jnp.float32(0.0625)
    fraction = jax.random.uniform(jax.random.fold_in(key, 7010), (H,), jnp.float32)
    return jnp.exp(jnp.log(lowest) + fraction * (jnp.log(highest) - jnp.log(lowest)))


def steps_of(key, shape, cuts, low, high):
    gain = 1.0
    for position, shards_of in cuts:
        steps = jax.random.uniform(jax.random.fold_in(jax.random.fold_in(key, 6), position), (shards_of,), jnp.float32, low / len(cuts), high / len(cuts))
        gain = gain * jnp.repeat(jnp.exp(steps), shape[position] // shards_of).reshape((-1,) + (1,) * (len(shape) - 1 - position))
    return gain


def length_profile(amount, total, most, lean):
    loads = [(1 << 20) // math.isqrt(grade ** lean) + 1 for grade in range(2, amount + 1)]
    rest, counts = total - most - (amount - 1), [1] * (amount - 1)
    while rest > 0:
        free = [i for i in range(amount - 1) if counts[i] < most]
        whole, left = sum([loads[i] for i in free]), rest
        for i in free:
            extra = min(most - counts[i], max(1, left * loads[i] // whole), rest)
            counts[i] = counts[i] + extra
            rest = rest - extra
    return np.array([most] + counts)


def ragged_sizes(stream_key, number_of, total, limit, slope):
    if number_of == 2:
        one = jax.random.randint(stream_key, (), max(1, total - limit), min(limit, total - 1) + 1)
        return jnp.stack([one, total - one])
    lengths = jnp.asarray(length_profile(number_of, total, limit, slope), jnp.int32)
    couples = (number_of - 1) // 2
    donor, taker = lengths[1:1 + 2 * couples:2], lengths[2:2 + 2 * couples:2]
    room = jnp.minimum(donor - 1, limit - taker)
    passed = jax.random.randint(jax.random.fold_in(stream_key, 1), (couples,), 0, 1 << 20) % (room + 1)
    lengths = lengths.at[1:1 + 2 * couples:2].set(donor - passed).at[2:2 + 2 * couples:2].set(taker + passed)
    return lengths[jax.random.permutation(jax.random.fold_in(stream_key, 2), number_of)]


def scatter_about(key, shape, spread, most, cuts=(), kind=jnp.bfloat16):
    result = spread * jax.random.normal(key, shape, jnp.float32)
    if cuts:
        result = result * steps_of(key, shape, cuts, -0.22, 0.18)
    return jnp.clip(result, -most, most).astype(kind)


def setup_inputs(seed: int = 0) -> dict:
    key_list = jax.random.split(jax.random.key(seed), 6)
    return {
        "query_states": draw_query_states(jax.random.fold_in(key_list[5], 71), 0),
        "key_states": draw_key_states(jax.random.fold_in(key_list[5], 71), 0),
        "value_states": scatter_about(key_list[2], (TOKENS, H * HD), 1.0, 6.0, ((0, 512),)),
        "doc_lengths": ragged_sizes(key_list[3], DOCS, TOKENS, DOC_MAX, 2).astype(jnp.int32),
        "slopes": draw_slopes(jax.random.fold_in(key_list[5], 71), 0),
    }


NEG_FILL = -1e+30

def reference(query_states, key_states, value_states, doc_lengths, slopes):
    boundary = jnp.cumsum(doc_lengths).astype(jnp.int32)
    positions = jnp.arange(TOKENS, dtype=jnp.int32)
    doc_index = lax.optimization_barrier(jnp.sum((boundary[None, :] <= positions[:, None]).astype(jnp.int32), axis=1))
    queries_all = query_states.reshape(TOKENS, H, HD)
    padded_keys = jnp.concatenate([jnp.zeros((DOC_MAX, H, HD), key_states.dtype), key_states.reshape(TOKENS, H, HD)], axis=0)
    padded_values = jnp.concatenate([jnp.zeros((DOC_MAX, H, HD), value_states.dtype), value_states.reshape(TOKENS, H, HD)], axis=0)
    padded_pos = jnp.arange(TOKENS + DOC_MAX, dtype=jnp.int32) - DOC_MAX
    padded_doc = jnp.concatenate([jnp.full((DOC_MAX,), -1, jnp.int32), doc_index])
    block_rows = 256 if TOKENS % 256 == 0 else TOK_DEV
    window = DOC_MAX + block_rows
    inv_root = 1.0 / math.sqrt(HD)

    def one_block(block_id):
        row_start = (block_id * block_rows).astype(jnp.int32)
        query_block = lax.dynamic_slice_in_dim(queries_all, row_start, block_rows, 0).astype(jnp.float32)
        query_pos = lax.dynamic_slice_in_dim(positions, row_start, block_rows, 0)
        query_doc = lax.dynamic_slice_in_dim(doc_index, row_start, block_rows, 0)
        key_block = lax.dynamic_slice_in_dim(padded_keys, row_start, window, 0).astype(jnp.float32)
        value_block = lax.dynamic_slice_in_dim(padded_values, row_start, window, 0).astype(jnp.float32)
        key_pos = lax.dynamic_slice_in_dim(padded_pos, row_start, window, 0)
        key_doc = lax.dynamic_slice_in_dim(padded_doc, row_start, window, 0)
        scores = jnp.einsum('qhd,khd->qhk', query_block, key_block, precision=lax.Precision.HIGHEST) * inv_root
        distance = (query_pos[:, None] - key_pos[None, :]).astype(jnp.float32)
        scores = scores - slopes[None, :, None] * distance[:, None, :]
        allowed = (query_doc[:, None] == key_doc[None, :]) & (key_pos[None, :] <= query_pos[:, None])
        scores = jnp.where(allowed[:, None, :], scores, NEG_FILL)
        row_max = lax.optimization_barrier(jnp.max(scores, axis=-1))
        weights = jnp.where(allowed[:, None, :], jnp.exp(scores - row_max[:, :, None]), 0.0)
        row_total = lax.optimization_barrier(jnp.sum(weights, axis=-1))
        rounded = lax.optimization_barrier(weights.astype(jnp.bfloat16)).astype(jnp.float32)
        numerator = jnp.einsum('qhk,khd->qhd', rounded, value_block, precision=lax.Precision.HIGHEST)
        return (numerator / row_total[:, :, None]).astype(jnp.bfloat16).reshape(block_rows, H * HD)
    blocks = lax.map(one_block, jnp.arange(TOKENS // block_rows, dtype=jnp.int32))
    return blocks.reshape(TOKENS, H * HD)
```

```python
import functools
import math

import jax
import jax.numpy as jnp
from jax import lax
from jax.experimental import pallas as pl
from jax.experimental.pallas import tpu as pltpu
from jax.sharding import PartitionSpec as P

AXES = ("outer", "inner")
TILE = 256
NEG_FILL = -1e30
LOG2E = math.log2(math.e)


def pack_kernel(heads, count, *refs):
    sources, out_ref = refs[:-1], refs[-1]
    groups = out_ref.shape[0]
    for group in range(groups):
        place = 0
        for source in sources:
            for head in heads:
                column = (group * count + head) * 128
                out_ref[group, :, place : place + 128] = source[:, column : column + 128]
                place += 128


def pack(sources, heads, count, groups):
    rows = sources[0].shape[0]
    width = len(sources) * len(heads) * 128
    return pl.pallas_call(
        functools.partial(pack_kernel, heads, count),
        out_shape=jax.ShapeDtypeStruct((groups, rows, width), jnp.bfloat16),
        in_specs=[pl.BlockSpec(memory_space=pltpu.VMEM)] * len(sources),
        out_specs=pl.BlockSpec(memory_space=pltpu.VMEM),
        compiler_params=pltpu.CompilerParams(vmem_limit_bytes=16 << 20),
        cost_estimate=pl.CostEstimate(
            flops=0, bytes_accessed=4 * groups * rows * width, transcendentals=0
        ),
    )(*sources)


def unpack_kernel(recv_ref, out_ref):
    groups, _, width = recv_ref.shape
    for group in range(groups):
        out_ref[:, group * width : (group + 1) * width] = recv_ref[group]


def unpack(recv):
    groups, rows, width = recv.shape
    return pl.pallas_call(
        unpack_kernel,
        out_shape=jax.ShapeDtypeStruct((rows, groups * width), jnp.bfloat16),
        in_specs=[pl.BlockSpec(memory_space=pltpu.VMEM)],
        out_specs=pl.BlockSpec(memory_space=pltpu.VMEM),
        compiler_params=pltpu.CompilerParams(vmem_limit_bytes=16 << 20),
    )(recv)


def attend_kernel(
    inv_root, first, tiles_ref, slopes_ref, start_ref, q_ref, kl_ref, vl_ref, kh_ref, vh_ref,
    out_ref, key_win, value_win,
):
    span = q_ref.shape[0]
    tiles = span // TILE
    most = span // TILE + 1

    @pl.when(pl.program_id(0) == 0)
    def _():
        value_win[:, 128:] = jnp.ones((2 * span, 128), jnp.bfloat16)

    key_win[:span, :] = kh_ref[...]
    key_win[span:, :] = kl_ref[...]
    value_win[:span, :128] = vh_ref[...]
    value_win[span:, :128] = vl_ref[...]
    slope = slopes_ref[first + pl.program_id(0)] * LOG2E

    def one_tile(tile, _):
        row = pl.multiple_of(tile * TILE, TILE)
        needed = tiles_ref[tile]

        for count in range(1, most + 1):

            @pl.when(needed == count)
            def _():
                width = count * TILE
                base = pl.multiple_of((tile + tiles + 1 - count) * TILE, TILE)
                scores = lax.dot_general(
                    q_ref[pl.ds(row, TILE), :],
                    key_win[pl.ds(base, width), :],
                    (((1,), (1,)), ((), ())),
                    preferred_element_type=jnp.float32,
                )
                offset = lax.broadcasted_iota(jnp.int32, (1, width), 1)
                bias = slope * (offset - width).astype(jnp.float32)
                scores = scores * (inv_root * LOG2E) + bias
                begin = start_ref[pl.ds(row, TILE), :] - base
                scores = jnp.where(offset >= begin, scores, NEG_FILL)
                row_in = lax.broadcasted_iota(jnp.int32, (TILE, TILE), 0)
                column_in = lax.broadcasted_iota(jnp.int32, (TILE, TILE), 1)
                last = jnp.where(column_in <= row_in, scores[:, width - TILE :], NEG_FILL)
                if count > 1:
                    scores = jnp.concatenate([scores[:, : width - TILE], last], axis=1)
                else:
                    scores = last
                row_max = jnp.max(scores, axis=1, keepdims=True)
                weights = jnp.exp2(scores - row_max).astype(jnp.bfloat16)
                both = lax.dot_general(
                    weights,
                    value_win[pl.ds(base, width), :],
                    (((1,), (0,)), ((), ())),
                    preferred_element_type=jnp.float32,
                )
                out_ref[pl.ds(row, TILE), :] = (both[:, :128] / both[:, 128:]).astype(
                    jnp.bfloat16
                )

        return 0

    lax.fori_loop(0, tiles, one_tile, 0)


def attend(tiles_needed, slopes, starts, queries, own, halo, first, heads, q_first):
    span = queries.shape[0]

    def columns(offset):
        return pl.BlockSpec((span, 128), lambda i: (0, offset + i))

    smem = pl.BlockSpec(memory_space=pltpu.SMEM)
    return pl.pallas_call(
        functools.partial(attend_kernel, 1.0 / math.sqrt(128), first),
        grid=(heads,),
        out_shape=jax.ShapeDtypeStruct((span, heads * 128), jnp.bfloat16),
        in_specs=[
            smem,
            smem,
            pl.BlockSpec((span, 1), lambda i: (0, 0)),
            columns(q_first),
            columns(0),
            columns(heads),
            columns(0),
            columns(heads),
        ],
        out_specs=columns(0),
        scratch_shapes=[
            pltpu.VMEM((2 * span, 128), jnp.bfloat16),
            pltpu.VMEM((2 * span, 256), jnp.bfloat16),
        ],
        compiler_params=pltpu.CompilerParams(vmem_limit_bytes=40 << 20),
        cost_estimate=pl.CostEstimate(
            flops=heads * 4 * span * (span + TILE) * 128,
            bytes_accessed=heads * span * 128 * 12,
            transcendentals=heads * span * (span + TILE),
        ),
    )(tiles_needed, slopes, starts, queries, own, own, halo, halo)


def per_device(query_states, key_states, value_states, doc_lengths, slopes):
    rows = query_states.shape[0]
    outer, inner = lax.axis_size("outer"), lax.axis_size("inner")
    groups = 2 * inner
    supers = outer * inner // groups
    span = groups * rows
    count = slopes.shape[0] // groups
    me = lax.axis_index("outer") * inner + lax.axis_index("inner")
    super_index, member = me // groups, me % groups
    index_groups = [[s * groups + m for m in range(groups)] for s in range(supers)]
    onward = [(i, i + groups) for i in range((supers - 1) * groups)]

    def exchange(value):
        got = lax.all_to_all(value, AXES, 0, 0, axis_index_groups=index_groups)
        return got.reshape(span, value.shape[-1])

    half = count // 2
    parts = [tuple(range(half)), tuple(range(half, count))]
    own, halo = [], []
    for heads in parts:
        own.append(exchange(pack([key_states, value_states], heads, count, groups)))
        halo.append(lax.ppermute(own[-1], AXES, onward))
    queries = exchange(pack([query_states], tuple(range(count)), count, groups))

    ids = jnp.arange(doc_lengths.shape[0])
    ends = jnp.sum(jnp.where(ids[:, None] <= ids[None, :], doc_lengths[:, None], 0), axis=0)
    position = super_index * span + jnp.arange(span, dtype=jnp.int32)
    starts = jnp.max(jnp.where(ends[None, :] <= position[:, None], ends[None, :], 0), axis=1)
    starts = starts - (super_index - 1) * span
    tiles = span // TILE
    needed = jnp.arange(tiles) + tiles + 1 - starts[::TILE] // TILE
    my_slopes = lax.dynamic_slice(slopes, (member * count,), (count,))

    outs = []
    for i, heads in enumerate(parts):
        outs.append(
            attend(
                needed, my_slopes, starts[:, None], queries, own[i], halo[i],
                heads[0], len(heads), heads[0],
            )
        )
    out = jnp.concatenate(outs, axis=1).reshape(groups, rows, count * 128)
    back = lax.all_to_all(out, AXES, 0, 0, axis_index_groups=index_groups)
    return unpack(back)


def solution(mesh):
    tokens = P(AXES, None)
    return jax.shard_map(
        per_device,
        mesh=mesh,
        in_specs=(tokens, tokens, tokens, P(), P()),
        out_specs=tokens,
        check_vma=False,
    )
```

```python
import functools
import math

import jax
import jax.numpy as jnp
from jax import lax
from jax.experimental import pallas as pl
from jax.experimental.pallas import tpu as pltpu
from jax.sharding import PartitionSpec as P

AXES = ("outer", "inner")
TILE = 256
NEG_FILL = -1e30
VMEM_BYTES = 60 << 20
LOG2E = math.log2(math.e)
IN_BATCHES = ((2, 0), (2, 0), (0, 4))
OUT_BATCHES = (2, 2)


def copy_all(copies):
    for copy in copies:
        copy.start()
    for copy in copies:
        copy.wait()


def pack_kernel(pieces, count, *refs):
    sources, (out_ref, stage, in_sems, out_sems) = refs[:-4], refs[-4:]
    groups = out_ref.shape[0]
    loads, stores = [], []
    for group in range(groups):
        place, mine = 0, []
        for i, (source, (head, heads)) in enumerate(zip(sources, pieces)):
            mine.append(
                pltpu.make_async_copy(
                    source.at[:, pl.ds((group * count + head) * 128, heads * 128)],
                    stage.at[group, :, pl.ds(place, heads * 128)],
                    in_sems.at[group, i],
                )
            )
            place += heads * 128
        loads.append(mine)
        stores.append(pltpu.make_async_copy(stage.at[group], out_ref.at[group], out_sems.at[group]))
    for mine in loads:
        for load in mine:
            load.start()
    for mine, store in zip(loads, stores):
        for load in mine:
            load.wait()
        store.start()
    for store in stores:
        store.wait()


def pack(sources, pieces, count, groups):
    rows = sources[0].shape[0]
    width = sum(heads for _, heads in pieces) * 128
    shape = (groups, rows, width)
    return pl.pallas_call(
        functools.partial(pack_kernel, pieces, count),
        out_shape=jax.ShapeDtypeStruct(shape, jnp.bfloat16),
        in_specs=[pl.BlockSpec(memory_space=pltpu.HBM)] * len(sources),
        out_specs=pl.BlockSpec(memory_space=pltpu.HBM),
        scratch_shapes=[
            pltpu.VMEM(shape, jnp.bfloat16),
            pltpu.SemaphoreType.DMA((groups, len(sources))),
            pltpu.SemaphoreType.DMA((groups,)),
        ],
        compiler_params=pltpu.CompilerParams(vmem_limit_bytes=VMEM_BYTES),
        cost_estimate=pl.CostEstimate(
            flops=0, bytes_accessed=4 * groups * rows * width, transcendentals=0
        ),
    )(*sources)


def unpack_kernel(count, *refs):
    parts, out_ref = refs[:-1], refs[-1]
    place = 0
    for part in parts:
        groups, _, width = part.shape
        for group in range(groups):
            column = group * count * 128 + place
            out_ref[:, column : column + width] = part[group]
        place += width


def unpack(parts, count):
    groups, rows = parts[0].shape[:2]
    return pl.pallas_call(
        functools.partial(unpack_kernel, count),
        out_shape=jax.ShapeDtypeStruct((rows, groups * count * 128), jnp.bfloat16),
        in_specs=[pl.BlockSpec(memory_space=pltpu.VMEM)] * len(parts),
        out_specs=pl.BlockSpec(memory_space=pltpu.VMEM),
        compiler_params=pltpu.CompilerParams(vmem_limit_bytes=16 << 20),
    )(*parts)


def attend_kernel(
    inv_root, first, q_place, out_place, tiles_ref, slopes_ref, firsts_ref, q_hbm, own_hbm, halo_hbm,
    *refs,
):
    out_hbm, q_all, both_win, value_win, out_all, sems = refs[-6:]
    span = q_all.shape[0]
    heads = q_all.shape[1] // 128
    tiles = span // TILE
    most = tiles + 1
    halves = [pl.ds(0, span), pl.ds(span, span)]
    copies = [
        pltpu.make_async_copy(
            own_hbm.at[:, pl.ds(0, 2 * heads * 128)], both_win.at[halves[1], :], sems.at[0]
        ),
        pltpu.make_async_copy(halo_hbm, both_win.at[halves[0], :], sems.at[1]),
        pltpu.make_async_copy(q_hbm.at[:, pl.ds(q_place * 128, heads * 128)], q_all, sems.at[2]),
    ]
    for copy in copies:
        copy.start()
    for head in range(heads):
        value_win[head, 128:, :] = jnp.ones((16, 2 * span), jnp.bfloat16)
    for copy, half in zip(copies, halves[::-1]):
        copy.wait()
        for head in range(heads):
            columns = slice((heads + head) * 128, (heads + head + 1) * 128)
            value_win[head, :128, half] = both_win[half, columns].T
    copies[2].wait()
    firsts = firsts_ref[...]

    def one_tile(tile, _):
        row = pl.multiple_of(tile * TILE, TILE)
        needed = tiles_ref[tile]
        at = lax.broadcasted_iota(jnp.int32, (128, TILE), 1) + (span + row)
        begin_all = jnp.max(jnp.where(firsts <= at, firsts, 0), axis=0, keepdims=True)

        for count in range(1, most + 1):

            @pl.when(needed == count)
            def _():
                width = count * TILE
                base = pl.multiple_of((tile + tiles + 1 - count) * TILE, TILE)
                begin = begin_all - base
                offset = lax.broadcasted_iota(jnp.int32, (width, TILE), 0)
                distance = (offset - width).astype(jnp.float32)
                key_in = lax.broadcasted_iota(jnp.int32, (TILE, TILE), 0)
                query_in = lax.broadcasted_iota(jnp.int32, (TILE, TILE), 1)
                in_document = offset >= begin
                past = key_in <= query_in
                all_scores = []
                for head in range(heads):
                    columns = slice(head * 128, (head + 1) * 128)
                    all_scores.append(
                        lax.dot_general(
                            both_win[pl.ds(base, width), columns],
                            q_all[pl.ds(row, TILE), columns],
                            (((1,), (1,)), ((), ())),
                            preferred_element_type=jnp.float32,
                        )
                    )
                for head, scores in enumerate(all_scores):
                    slope = slopes_ref[first + head] * LOG2E
                    scores = scores * (inv_root * LOG2E) + slope * distance
                    scores = jnp.where(in_document, scores, NEG_FILL)
                    last = jnp.where(past, scores[width - TILE :], NEG_FILL)
                    if count > 1:
                        scores = jnp.concatenate([scores[: width - TILE], last], axis=0)
                    else:
                        scores = last
                    all_scores[head] = scores
                all_weights = []
                for scores in all_scores:
                    row_max = jnp.max(scores, axis=0, keepdims=True)
                    all_weights.append(jnp.exp2(scores - row_max).astype(jnp.bfloat16))
                for head, weights in enumerate(all_weights):
                    columns = slice(head * 128, (head + 1) * 128)
                    both = lax.dot_general(
                        value_win[head, :, pl.ds(base, width)],
                        weights,
                        (((1,), (0,)), ((), ())),
                        preferred_element_type=jnp.float32,
                    )
                    result = both[:128] * (1.0 / both[128:129])
                    out_all[pl.ds(row, TILE), columns] = result.T.astype(jnp.bfloat16)

        return 0

    lax.fori_loop(0, tiles, one_tile, 0)
    place = pl.ds(out_place * 128, heads * 128)
    copy_all([pltpu.make_async_copy(out_all, out_hbm.at[:, place], sems.at[0])])


def attend(
    tiles_needed, slopes, firsts, queries, own, halo, first, heads, q_place, before, out_heads, out_place
):
    span = queries.shape[0]
    smem = pl.BlockSpec(memory_space=pltpu.SMEM)
    hbm = pl.BlockSpec(memory_space=pltpu.HBM)
    more = [] if before is None else [before]
    return pl.pallas_call(
        functools.partial(attend_kernel, 1.0 / math.sqrt(128), first, q_place, out_place),
        out_shape=jax.ShapeDtypeStruct((span, out_heads * 128), jnp.bfloat16),
        in_specs=[smem, smem, pl.BlockSpec(memory_space=pltpu.VMEM), hbm, hbm, hbm]
        + [pl.BlockSpec(memory_space=pltpu.HBM)] * len(more),
        out_specs=pl.BlockSpec(memory_space=pltpu.HBM),
        input_output_aliases={6: 0} if more else {},
        scratch_shapes=[
            pltpu.VMEM((span, heads * 128), jnp.bfloat16),
            pltpu.VMEM((2 * span, 2 * heads * 128), jnp.bfloat16),
            pltpu.VMEM((heads, 144, 2 * span), jnp.bfloat16),
            pltpu.VMEM((span, heads * 128), jnp.bfloat16),
            pltpu.SemaphoreType.DMA((3,)),
        ],
        compiler_params=pltpu.CompilerParams(vmem_limit_bytes=40 << 20),
        cost_estimate=pl.CostEstimate(
            flops=heads * 4 * span * (span + TILE) * 128,
            bytes_accessed=heads * span * 128 * 12,
            transcendentals=heads * span * (span + TILE),
        ),
    )(tiles_needed, slopes, firsts, queries, own, halo, *more)


def per_device(query_states, key_states, value_states, doc_lengths, slopes):
    rows = query_states.shape[0]
    outer, inner = lax.axis_size("outer"), lax.axis_size("inner")
    groups = 2 * inner
    supers = outer * inner // groups
    span = groups * rows
    count = slopes.shape[0] // groups
    me = lax.axis_index("outer") * inner + lax.axis_index("inner")
    super_index, member = me // groups, me % groups
    index_groups = [[s * groups + m for m in range(groups)] for s in range(supers)]
    onward = [(i, i + groups) for i in range((supers - 1) * groups)]

    def exchange(value):
        got = lax.all_to_all(value, AXES, 0, 0, axis_index_groups=index_groups)
        return got.reshape(span, value.shape[-1])

    own, halo, first_of, queries = [], [], [], {}
    next_kv, next_q = 0, 0
    for kv, q in IN_BATCHES:
        pieces = [(key_states, (next_kv, kv)), (value_states, (next_kv, kv))] * (kv > 0)
        pieces += [(query_states, (next_q, q))] * (q > 0)
        packed = pack([p[0] for p in pieces], tuple(p[1] for p in pieces), count, groups)
        got = exchange(packed)
        if kv:
            own.append(got)
            halo.append(lax.ppermute(got[:, : 2 * kv * 128], AXES, onward))
            first_of.append((next_kv, kv))
        for i in range(q):
            queries[next_q + i] = (got, 2 * kv + i)
        next_kv, next_q = next_kv + kv, next_q + q

    ids = jnp.arange(doc_lengths.shape[0])
    firsts = jnp.sum(jnp.where(ids[:, None] < ids[None, :], doc_lengths[:, None], 0), axis=0)
    firsts = firsts - (super_index - 1) * span
    tiles = span // TILE
    block = jnp.arange(tiles, dtype=jnp.int32)
    starts = jnp.max(jnp.where(firsts[None, :] <= (span + block * TILE)[:, None], firsts[None, :], 0), axis=1)
    needed = block + tiles + 1 - starts // TILE
    my_slopes = lax.dynamic_slice(slopes, (member * count,), (count,))

    outs, done, place, batch = [], None, 0, 0
    for i, (first, heads) in enumerate(first_of):
        asked, q_place = queries[first]
        done = attend(
            needed, my_slopes, firsts[:, None], asked, own[i], halo[i], first, heads, q_place,
            done, OUT_BATCHES[batch], place,
        )
        place += heads
        if place == OUT_BATCHES[batch]:
            done = done.reshape(groups, rows, place * 128)
            outs.append(lax.all_to_all(done, AXES, 0, 0, axis_index_groups=index_groups))
            done, place, batch = None, 0, batch + 1
    return unpack(outs, count)


def solution(mesh):
    tokens = P(AXES, None)
    return jax.shard_map(
        per_device,
        mesh=mesh,
        in_specs=(tokens, tokens, tokens, P(), P()),
        out_specs=tokens,
        check_vma=False,
    )
```

```python
import functools
import math

import jax
import jax.numpy as jnp
from jax import lax
from jax.experimental import pallas as pl
from jax.experimental.pallas import tpu as pltpu
from jax.sharding import PartitionSpec as P

AXES = ("outer", "inner")
TILE = 256
NEG_FILL = -1e30
VMEM_BYTES = 60 << 20
LOG2E = math.log2(math.e)
IN_BATCHES = ((2, 0), (2, 0), (0, 4))


def copy_all(copies):
    for copy in copies:
        copy.start()
    for copy in copies:
        copy.wait()


def pack_kernel(pieces, count, *refs):
    sources, (out_ref, stage, in_sems, out_sems) = refs[:-4], refs[-4:]
    groups = out_ref.shape[0]
    loads, stores = [], []
    for group in range(groups):
        place, mine = 0, []
        for i, (source, (head, heads)) in enumerate(zip(sources, pieces)):
            mine.append(
                pltpu.make_async_copy(
                    source.at[:, pl.ds((group * count + head) * 128, heads * 128)],
                    stage.at[group, :, pl.ds(place, heads * 128)],
                    in_sems.at[group, i],
                )
            )
            place += heads * 128
        loads.append(mine)
        stores.append(pltpu.make_async_copy(stage.at[group], out_ref.at[group], out_sems.at[group]))
    for mine in loads:
        for load in mine:
            load.start()
    for mine, store in zip(loads, stores):
        for load in mine:
            load.wait()
        store.start()
    for store in stores:
        store.wait()


def pack(sources, pieces, count, groups):
    rows = sources[0].shape[0]
    width = sum(heads for _, heads in pieces) * 128
    shape = (groups, rows, width)
    return pl.pallas_call(
        functools.partial(pack_kernel, pieces, count),
        out_shape=jax.ShapeDtypeStruct(shape, jnp.bfloat16),
        in_specs=[pl.BlockSpec(memory_space=pltpu.HBM)] * len(sources),
        out_specs=pl.BlockSpec(memory_space=pltpu.HBM),
        scratch_shapes=[
            pltpu.VMEM(shape, jnp.bfloat16),
            pltpu.SemaphoreType.DMA((groups, len(sources))),
            pltpu.SemaphoreType.DMA((groups,)),
        ],
        compiler_params=pltpu.CompilerParams(vmem_limit_bytes=VMEM_BYTES),
        cost_estimate=pl.CostEstimate(
            flops=0, bytes_accessed=4 * groups * rows * width, transcendentals=0
        ),
    )(*sources)


def unpack_kernel(count, *refs):
    parts, out_ref = refs[:-1], refs[-1]
    place = 0
    for part in parts:
        groups, _, width = part.shape
        for group in range(groups):
            column = group * count * 128 + place
            out_ref[:, column : column + width] = part[group]
        place += width


def unpack(parts, count):
    groups, rows = parts[0].shape[:2]
    return pl.pallas_call(
        functools.partial(unpack_kernel, count),
        out_shape=jax.ShapeDtypeStruct((rows, groups * count * 128), jnp.bfloat16),
        in_specs=[pl.BlockSpec(memory_space=pltpu.VMEM)] * len(parts),
        out_specs=pl.BlockSpec(memory_space=pltpu.VMEM),
        compiler_params=pltpu.CompilerParams(vmem_limit_bytes=16 << 20),
    )(*parts)


def attend_kernel(
    inv_root, first, q_place, tiles_ref, slopes_ref, firsts_ref, q_ref, own_ref, halo_hbm,
    out_ref, key_win, value_win, stage, sems,
):
    span = q_ref.shape[0]
    heads = out_ref.shape[1] // 128
    tiles = span // TILE
    most = tiles + 1
    wide = heads * 128
    before, mine = pl.ds(0, span), pl.ds(span, span)
    copies = [
        pltpu.make_async_copy(halo_hbm.at[:, pl.ds(wide, wide)], stage, sems.at[0]),
        pltpu.make_async_copy(halo_hbm.at[:, pl.ds(0, wide)], key_win.at[before, :], sems.at[1]),
    ]
    for copy in copies:
        copy.start()
    key_win[mine, :] = own_ref[:, :wide]
    for head in range(heads):
        columns = slice(head * 128, (head + 1) * 128)
        value_win[head, 128:, :] = jnp.ones((16, 2 * span), jnp.bfloat16)
        value_win[head, :128, mine] = own_ref[:, wide + head * 128 : wide + (head + 1) * 128].T
    copies[0].wait()
    for head in range(heads):
        value_win[head, :128, before] = stage[:, head * 128 : (head + 1) * 128].T
    copies[1].wait()
    firsts = firsts_ref[...]

    def one_tile(tile, _):
        row = pl.multiple_of(tile * TILE, TILE)
        needed = tiles_ref[tile]
        at = lax.broadcasted_iota(jnp.int32, (128, TILE), 1) + (span + row)
        begin_all = jnp.max(jnp.where(firsts <= at, firsts, 0), axis=0, keepdims=True)

        for count in range(1, most + 1):

            @pl.when(needed == count)
            def _():
                width = count * TILE
                base = pl.multiple_of((tile + tiles + 1 - count) * TILE, TILE)
                begin = begin_all - base
                offset = lax.broadcasted_iota(jnp.int32, (width, TILE), 0)
                distance = (offset - width).astype(jnp.float32)
                key_in = lax.broadcasted_iota(jnp.int32, (TILE, TILE), 0)
                query_in = lax.broadcasted_iota(jnp.int32, (TILE, TILE), 1)
                in_document = offset >= begin
                past = key_in <= query_in
                all_scores = []
                for head in range(heads):
                    columns = slice(head * 128, (head + 1) * 128)
                    all_scores.append(
                        lax.dot_general(
                            key_win[pl.ds(base, width), columns],
                            q_ref[pl.ds(row, TILE), pl.ds((q_place + head) * 128, 128)],
                            (((1,), (1,)), ((), ())),
                            preferred_element_type=jnp.float32,
                        )
                    )
                for head, scores in enumerate(all_scores):
                    slope = slopes_ref[first + head] * LOG2E
                    scores = scores * (inv_root * LOG2E) + slope * distance
                    scores = jnp.where(in_document, scores, NEG_FILL)
                    last = jnp.where(past, scores[width - TILE :], NEG_FILL)
                    if count > 1:
                        scores = jnp.concatenate([scores[: width - TILE], last], axis=0)
                    else:
                        scores = last
                    all_scores[head] = scores
                all_weights = []
                for scores in all_scores:
                    row_max = jnp.max(scores, axis=0, keepdims=True)
                    all_weights.append(jnp.exp2(scores - row_max).astype(jnp.bfloat16))
                for head, weights in enumerate(all_weights):
                    columns = slice(head * 128, (head + 1) * 128)
                    both = lax.dot_general(
                        value_win[head, :, pl.ds(base, width)],
                        weights,
                        (((1,), (0,)), ((), ())),
                        preferred_element_type=jnp.float32,
                    )
                    result = both[:128] * (1.0 / both[128:129])
                    out_ref[pl.ds(row, TILE), columns] = result.T.astype(jnp.bfloat16)

        return 0

    lax.fori_loop(0, tiles, one_tile, 0)


def attend(tiles_needed, slopes, firsts, queries, own, halo, first, heads, q_place):
    span = queries.shape[0]
    smem = pl.BlockSpec(memory_space=pltpu.SMEM)
    vmem = pl.BlockSpec(memory_space=pltpu.VMEM)
    return pl.pallas_call(
        functools.partial(attend_kernel, 1.0 / math.sqrt(128), first, q_place),
        out_shape=jax.ShapeDtypeStruct((span, heads * 128), jnp.bfloat16),
        in_specs=[smem, smem, vmem, vmem, vmem, pl.BlockSpec(memory_space=pltpu.HBM)],
        out_specs=vmem,
        scratch_shapes=[
            pltpu.VMEM((2 * span, heads * 128), jnp.bfloat16),
            pltpu.VMEM((heads, 144, 2 * span), jnp.bfloat16),
            pltpu.VMEM((span, heads * 128), jnp.bfloat16),
            pltpu.SemaphoreType.DMA((2,)),
        ],
        compiler_params=pltpu.CompilerParams(vmem_limit_bytes=32 << 20),
        cost_estimate=pl.CostEstimate(
            flops=heads * 4 * span * (span + TILE) * 128,
            bytes_accessed=heads * span * 128 * 12,
            transcendentals=heads * span * (span + TILE),
        ),
    )(tiles_needed, slopes, firsts, queries, own, halo)


def own_kernel(
    inv_root, first, q_place, tiles_ref, slopes_ref, firsts_ref, q_ref, own_ref, earlier_ref,
    part_ref, value_win,
):
    span = q_ref.shape[0]
    heads = part_ref.shape[0]
    tiles = span // TILE
    wide = heads * 128
    for head in range(heads):
        value_win[head, 128:, :] = jnp.ones((16, span), jnp.bfloat16)
        value_win[head, :128, :] = own_ref[:, wide + head * 128 : wide + (head + 1) * 128].T
    firsts = firsts_ref[...]

    def one_tile(tile, _):
        row = pl.multiple_of(tile * TILE, TILE)
        needed = jnp.minimum(tiles_ref[tile], tile + 1)
        at = lax.broadcasted_iota(jnp.int32, (128, TILE), 1) + (span + row)
        begin_all = jnp.max(jnp.where(firsts <= at, firsts, 0), axis=0, keepdims=True)

        for count in range(1, tiles + 1):

            @pl.when(needed == count)
            def _():
                width = count * TILE
                base = pl.multiple_of((tile + 1 - count) * TILE, TILE)
                begin = begin_all - span - base
                offset = lax.broadcasted_iota(jnp.int32, (width, TILE), 0)
                distance = (offset - width).astype(jnp.float32)
                key_in = lax.broadcasted_iota(jnp.int32, (TILE, TILE), 0)
                query_in = lax.broadcasted_iota(jnp.int32, (TILE, TILE), 1)
                in_document = offset >= begin
                past = key_in <= query_in
                all_scores = []
                for head in range(heads):
                    all_scores.append(
                        lax.dot_general(
                            own_ref[pl.ds(base, width), head * 128 : (head + 1) * 128],
                            q_ref[pl.ds(row, TILE), pl.ds((q_place + head) * 128, 128)],
                            (((1,), (1,)), ((), ())),
                            preferred_element_type=jnp.float32,
                        )
                    )
                for head, scores in enumerate(all_scores):
                    slope = slopes_ref[first + head] * LOG2E
                    scores = scores * (inv_root * LOG2E) + slope * distance
                    scores = jnp.where(in_document, scores, NEG_FILL)
                    last = jnp.where(past, scores[width - TILE :], NEG_FILL)
                    if count > 1:
                        scores = jnp.concatenate([scores[: width - TILE], last], axis=0)
                    else:
                        scores = last
                    all_scores[head] = scores
                tops = [jnp.max(scores, axis=0, keepdims=True) for scores in all_scores]
                all_weights = [
                    jnp.exp2(scores - top).astype(jnp.bfloat16)
                    for scores, top in zip(all_scores, tops)
                ]
                for head, weights in enumerate(all_weights):
                    both = lax.dot_general(
                        value_win[head, :, pl.ds(base, width)],
                        weights,
                        (((1,), (0,)), ((), ())),
                        preferred_element_type=jnp.float32,
                    )
                    part_ref[head, :136, pl.ds(row, TILE)] = both[:136]
                    part_ref[head, 136:, pl.ds(row, TILE)] = jnp.broadcast_to(tops[head], (8, TILE))

        return 0

    lax.fori_loop(0, tiles, one_tile, 0)


def attend_own(tiles_needed, slopes, firsts, queries, own, earlier, first, heads, q_place):
    span = queries.shape[0]
    smem = pl.BlockSpec(memory_space=pltpu.SMEM)
    vmem = pl.BlockSpec(memory_space=pltpu.VMEM)
    return pl.pallas_call(
        functools.partial(own_kernel, 1.0 / math.sqrt(128), first, q_place),
        out_shape=jax.ShapeDtypeStruct((heads, 144, span), jnp.float32),
        in_specs=[smem, smem, vmem, vmem, vmem, pl.BlockSpec(memory_space=pl.ANY)],
        out_specs=vmem,
        scratch_shapes=[pltpu.VMEM((heads, 144, span), jnp.bfloat16)],
        compiler_params=pltpu.CompilerParams(vmem_limit_bytes=32 << 20),
        cost_estimate=pl.CostEstimate(
            flops=heads * 2 * span * (span + TILE) * 128,
            bytes_accessed=heads * span * 128 * 10,
            transcendentals=heads * span * (span + TILE) // 2,
        ),
    )(tiles_needed, slopes, firsts, queries, own, earlier)


def halo_kernel(
    inv_root, first, q_place, tiles_ref, slopes_ref, firsts_ref, q_ref, part_ref, halo_hbm,
    out_ref, key_win, value_win, stage, sems,
):
    span = q_ref.shape[0]
    heads = part_ref.shape[0]
    tiles = span // TILE
    wide = heads * 128
    copies = [
        pltpu.make_async_copy(halo_hbm.at[:, pl.ds(wide, wide)], stage, sems.at[0]),
        pltpu.make_async_copy(halo_hbm.at[:, pl.ds(0, wide)], key_win, sems.at[1]),
    ]
    for copy in copies:
        copy.start()
    for head in range(heads):
        value_win[head, 128:, :] = jnp.ones((16, span), jnp.bfloat16)
    copies[0].wait()
    for head in range(heads):
        value_win[head, :128, :] = stage[:, head * 128 : (head + 1) * 128].T
    copies[1].wait()
    firsts = firsts_ref[...]

    def one_tile(tile, _):
        row = pl.multiple_of(tile * TILE, TILE)
        needed = tiles_ref[tile] - (tile + 1)
        at = lax.broadcasted_iota(jnp.int32, (128, TILE), 1) + (span + row)
        begin_all = jnp.max(jnp.where(firsts <= at, firsts, 0), axis=0, keepdims=True)
        ahead = ((tile + 1) * TILE).astype(jnp.float32)

        def finish(head, sums, total):
            columns = slice(head * 128, (head + 1) * 128)
            result = sums * (1.0 / total)
            out_ref[pl.ds(row, TILE), columns] = result.T.astype(jnp.bfloat16)

        @pl.when(needed <= 0)
        def _():
            for head in range(heads):
                finish(
                    head,
                    part_ref[head, :128, pl.ds(row, TILE)],
                    part_ref[head, 128:129, pl.ds(row, TILE)],
                )

        for count in range(1, tiles + 1):

            @pl.when(needed == count)
            def _():
                width = count * TILE
                base = span - width
                offset = lax.broadcasted_iota(jnp.int32, (width, TILE), 0)
                distance = (offset - width).astype(jnp.float32) - ahead
                in_document = offset >= begin_all - base
                all_scores = []
                for head in range(heads):
                    all_scores.append(
                        lax.dot_general(
                            key_win[base:, head * 128 : (head + 1) * 128],
                            q_ref[pl.ds(row, TILE), pl.ds((q_place + head) * 128, 128)],
                            (((1,), (1,)), ((), ())),
                            preferred_element_type=jnp.float32,
                        )
                    )
                for head, scores in enumerate(all_scores):
                    slope = slopes_ref[first + head] * LOG2E
                    scores = scores * (inv_root * LOG2E) + slope * distance
                    all_scores[head] = jnp.where(in_document, scores, NEG_FILL)
                olds = [part_ref[head, 136:137, pl.ds(row, TILE)] for head in range(heads)]
                tops = [
                    jnp.maximum(old, jnp.max(scores, axis=0, keepdims=True))
                    for old, scores in zip(olds, all_scores)
                ]
                all_weights = [
                    jnp.exp2(scores - top).astype(jnp.bfloat16)
                    for scores, top in zip(all_scores, tops)
                ]
                for head, weights in enumerate(all_weights):
                    both = lax.dot_general(
                        value_win[head, :, base:],
                        weights,
                        (((1,), (0,)), ((), ())),
                        preferred_element_type=jnp.float32,
                    )
                    rescale = jnp.exp2(olds[head] - tops[head])
                    finish(
                        head,
                        both[:128] + rescale * part_ref[head, :128, pl.ds(row, TILE)],
                        both[128:129] + rescale * part_ref[head, 128:129, pl.ds(row, TILE)],
                    )

        return 0

    lax.fori_loop(0, tiles, one_tile, 0)


def attend_halo(tiles_needed, slopes, firsts, queries, part, halo, first, heads, q_place):
    span = queries.shape[0]
    smem = pl.BlockSpec(memory_space=pltpu.SMEM)
    vmem = pl.BlockSpec(memory_space=pltpu.VMEM)
    return pl.pallas_call(
        functools.partial(halo_kernel, 1.0 / math.sqrt(128), first, q_place),
        out_shape=jax.ShapeDtypeStruct((span, heads * 128), jnp.bfloat16),
        in_specs=[smem, smem, vmem, vmem, vmem, pl.BlockSpec(memory_space=pltpu.HBM)],
        out_specs=vmem,
        scratch_shapes=[
            pltpu.VMEM((span, heads * 128), jnp.bfloat16),
            pltpu.VMEM((heads, 144, span), jnp.bfloat16),
            pltpu.VMEM((span, heads * 128), jnp.bfloat16),
            pltpu.SemaphoreType.DMA((2,)),
        ],
        compiler_params=pltpu.CompilerParams(vmem_limit_bytes=32 << 20),
        cost_estimate=pl.CostEstimate(
            flops=heads * 2 * span * (span + TILE) * 128,
            bytes_accessed=heads * span * 128 * 10,
            transcendentals=heads * span * (span + TILE) // 2,
        ),
    )(tiles_needed, slopes, firsts, queries, part, halo)


def follow_kernel(value_ref, earlier_ref, out_ref):
    pass


def follow(value, earlier):
    anywhere = pl.BlockSpec(memory_space=pl.ANY)
    return pl.pallas_call(
        follow_kernel,
        out_shape=jax.ShapeDtypeStruct(value.shape, value.dtype),
        in_specs=[anywhere, anywhere],
        out_specs=anywhere,
        input_output_aliases={0: 0},
        compiler_params=pltpu.CompilerParams(vmem_limit_bytes=1 << 20),
    )(value, earlier)


def per_device(query_states, key_states, value_states, doc_lengths, slopes):
    rows = query_states.shape[0]
    outer, inner = lax.axis_size("outer"), lax.axis_size("inner")
    groups = 2 * inner
    supers = outer * inner // groups
    span = groups * rows
    count = slopes.shape[0] // groups
    me = lax.axis_index("outer") * inner + lax.axis_index("inner")
    super_index, member = me // groups, me % groups
    index_groups = [[s * groups + m for m in range(groups)] for s in range(supers)]
    onward = [(i, i + groups) for i in range((supers - 1) * groups)]

    def exchange(value):
        got = lax.all_to_all(value, AXES, 0, 0, axis_index_groups=index_groups)
        return got.reshape(span, value.shape[-1])

    own, halo, first_of, queries = [], [], [], {}
    next_kv, next_q = 0, 0
    for kv, q in IN_BATCHES:
        pieces = [(key_states, (next_kv, kv)), (value_states, (next_kv, kv))] * (kv > 0)
        pieces += [(query_states, (next_q, q))] * (q > 0)
        packed = pack([p[0] for p in pieces], tuple(p[1] for p in pieces), count, groups)
        got = exchange(packed)
        if kv:
            own.append(got)
            halo.append(lax.ppermute(got[:, : 2 * kv * 128], AXES, onward))
            first_of.append((next_kv, kv))
        for i in range(q):
            queries[next_q + i] = (got, 2 * kv + i)
        next_kv, next_q = next_kv + kv, next_q + q

    ids = jnp.arange(doc_lengths.shape[0])
    firsts = jnp.sum(jnp.where(ids[:, None] < ids[None, :], doc_lengths[:, None], 0), axis=0)
    firsts = firsts - (super_index - 1) * span
    tiles = span // TILE
    block = jnp.arange(tiles, dtype=jnp.int32)
    starts = jnp.max(jnp.where(firsts[None, :] <= (span + block * TILE)[:, None], firsts[None, :], 0), axis=1)
    needed = block + tiles + 1 - starts // TILE
    my_slopes = lax.dynamic_slice(slopes, (member * count,), (count,))

    outs = []
    for i, (first, heads) in enumerate(first_of):
        asked, q_place = queries[first]
        about = (needed, my_slopes, firsts[:, None], asked)
        if i == 0:
            done = attend(*about, own[i], halo[i], first, heads, q_place)
        else:
            part = attend_own(*about, own[i], own[i], first, heads, q_place)
            done = attend_halo(*about, part, halo[i], first, heads, q_place)
        sent = done.reshape(groups, rows, heads * 128)
        if outs:
            sent = follow(sent, outs[-1])
        outs.append(lax.all_to_all(sent, AXES, 0, 0, axis_index_groups=index_groups))
    return unpack(outs, count)


def solution(mesh):
    tokens = P(AXES, None)
    return jax.shard_map(
        per_device,
        mesh=mesh,
        in_specs=(tokens, tokens, tokens, P(), P()),
        out_specs=tokens,
        check_vma=False,
    )
```

```python
import functools
import math

import jax
import jax.numpy as jnp
from jax import lax
from jax.experimental import pallas as pl
from jax.experimental.pallas import tpu as pltpu
from jax.sharding import PartitionSpec as P

AXES = ("outer", "inner")
TILE = 256
NEG_FILL = -1e30
VMEM_BYTES = 60 << 20
LOG2E = math.log2(math.e)
IN_BATCHES = ((2, 0), (2, 0), (0, 4))


def copy_all(copies):
    for copy in copies:
        copy.start()
    for copy in copies:
        copy.wait()


def pack_kernel(pieces, count, *refs):
    sources, (out_ref, stage, in_sems, out_sems) = refs[:-4], refs[-4:]
    groups = out_ref.shape[0]
    loads, stores = [], []
    for group in range(groups):
        place, mine = 0, []
        for i, (source, (head, heads)) in enumerate(zip(sources, pieces)):
            mine.append(
                pltpu.make_async_copy(
                    source.at[:, pl.ds((group * count + head) * 128, heads * 128)],
                    stage.at[group, :, pl.ds(place, heads * 128)],
                    in_sems.at[group, i],
                )
            )
            place += heads * 128
        loads.append(mine)
        stores.append(pltpu.make_async_copy(stage.at[group], out_ref.at[group], out_sems.at[group]))
    for mine in loads:
        for load in mine:
            load.start()
    for mine, store in zip(loads, stores):
        for load in mine:
            load.wait()
        store.start()
    for store in stores:
        store.wait()


def pack(sources, pieces, count, groups):
    rows = sources[0].shape[0]
    width = sum(heads for _, heads in pieces) * 128
    shape = (groups, rows, width)
    return pl.pallas_call(
        functools.partial(pack_kernel, pieces, count),
        out_shape=jax.ShapeDtypeStruct(shape, jnp.bfloat16),
        in_specs=[pl.BlockSpec(memory_space=pltpu.HBM)] * len(sources),
        out_specs=pl.BlockSpec(memory_space=pltpu.HBM),
        scratch_shapes=[
            pltpu.VMEM(shape, jnp.bfloat16),
            pltpu.SemaphoreType.DMA((groups, len(sources))),
            pltpu.SemaphoreType.DMA((groups,)),
        ],
        compiler_params=pltpu.CompilerParams(vmem_limit_bytes=VMEM_BYTES),
        cost_estimate=pl.CostEstimate(
            flops=0, bytes_accessed=4 * groups * rows * width, transcendentals=0
        ),
    )(*sources)


def unpack_kernel(count, *refs):
    parts, out_ref = refs[:-1], refs[-1]
    place = 0
    for part in parts:
        groups, _, width = part.shape
        for group in range(groups):
            column = group * count * 128 + place
            out_ref[:, column : column + width] = part[group]
        place += width


def unpack(parts, count):
    groups, rows = parts[0].shape[:2]
    return pl.pallas_call(
        functools.partial(unpack_kernel, count),
        out_shape=jax.ShapeDtypeStruct((rows, groups * count * 128), jnp.bfloat16),
        in_specs=[pl.BlockSpec(memory_space=pltpu.VMEM)] * len(parts),
        out_specs=pl.BlockSpec(memory_space=pltpu.VMEM),
        compiler_params=pltpu.CompilerParams(vmem_limit_bytes=16 << 20),
    )(*parts)


def attend_kernel(
    inv_root, first, q_place, tiles_ref, slopes_ref, firsts_ref, q_ref, own_ref, halo_ref,
    out_ref, key_win, value_win,
):
    span = q_ref.shape[0]
    heads = out_ref.shape[1] // 128
    tiles = span // TILE
    most = tiles + 1
    wide = heads * 128
    before, mine = pl.ds(0, span), pl.ds(span, span)
    key_win[before, :] = halo_ref[:, :wide]
    key_win[mine, :] = own_ref[:, :wide]
    for head in range(heads):
        columns = slice(head * 128, (head + 1) * 128)
        value_win[head, 128:, :] = jnp.ones((16, 2 * span), jnp.bfloat16)
        value_win[head, :128, mine] = own_ref[:, wide + head * 128 : wide + (head + 1) * 128].T
        value_win[head, :128, before] = halo_ref[:, wide + head * 128 : wide + (head + 1) * 128].T
    firsts = firsts_ref[...]

    def one_tile(tile, _):
        row = pl.multiple_of(tile * TILE, TILE)
        needed = tiles_ref[tile]
        at = lax.broadcasted_iota(jnp.int32, (128, TILE), 1) + (span + row)
        begin_all = jnp.max(jnp.where(firsts <= at, firsts, 0), axis=0, keepdims=True)

        for count in range(1, most + 1):

            @pl.when(needed == count)
            def _():
                width = count * TILE
                base = pl.multiple_of((tile + tiles + 1 - count) * TILE, TILE)
                begin = begin_all - base
                offset = lax.broadcasted_iota(jnp.int32, (width, TILE), 0)
                distance = (offset - width).astype(jnp.float32)
                key_in = lax.broadcasted_iota(jnp.int32, (TILE, TILE), 0)
                query_in = lax.broadcasted_iota(jnp.int32, (TILE, TILE), 1)
                in_document = offset >= begin
                past = key_in <= query_in
                all_scores = []
                for head in range(heads):
                    columns = slice(head * 128, (head + 1) * 128)
                    all_scores.append(
                        lax.dot_general(
                            key_win[pl.ds(base, width), columns],
                            q_ref[pl.ds(row, TILE), pl.ds((q_place + head) * 128, 128)],
                            (((1,), (1,)), ((), ())),
                            preferred_element_type=jnp.float32,
                        )
                    )
                for head, scores in enumerate(all_scores):
                    slope = slopes_ref[first + head] * LOG2E
                    scores = scores * (inv_root * LOG2E) + slope * distance
                    scores = jnp.where(in_document, scores, NEG_FILL)
                    last = jnp.where(past, scores[width - TILE :], NEG_FILL)
                    if count > 1:
                        scores = jnp.concatenate([scores[: width - TILE], last], axis=0)
                    else:
                        scores = last
                    all_scores[head] = scores
                all_weights = []
                for scores in all_scores:
                    row_max = jnp.max(scores, axis=0, keepdims=True)
                    all_weights.append(jnp.exp2(scores - row_max).astype(jnp.bfloat16))
                for head, weights in enumerate(all_weights):
                    columns = slice(head * 128, (head + 1) * 128)
                    both = lax.dot_general(
                        value_win[head, :, pl.ds(base, width)],
                        weights,
                        (((1,), (0,)), ((), ())),
                        preferred_element_type=jnp.float32,
                    )
                    result = both[:128] * (1.0 / both[128:129])
                    out_ref[pl.ds(row, TILE), columns] = result.T.astype(jnp.bfloat16)

        return 0

    lax.fori_loop(0, tiles, one_tile, 0)


def attend(tiles_needed, slopes, firsts, queries, own, halo, first, heads, q_place):
    span = queries.shape[0]
    smem = pl.BlockSpec(memory_space=pltpu.SMEM)
    vmem = pl.BlockSpec(memory_space=pltpu.VMEM)
    return pl.pallas_call(
        functools.partial(attend_kernel, 1.0 / math.sqrt(128), first, q_place),
        out_shape=jax.ShapeDtypeStruct((span, heads * 128), jnp.bfloat16),
        in_specs=[smem, smem, vmem, vmem, vmem, vmem],
        out_specs=vmem,
        scratch_shapes=[
            pltpu.VMEM((2 * span, heads * 128), jnp.bfloat16),
            pltpu.VMEM((heads, 144, 2 * span), jnp.bfloat16),
        ],
        compiler_params=pltpu.CompilerParams(vmem_limit_bytes=32 << 20),
        cost_estimate=pl.CostEstimate(
            flops=heads * 4 * span * (span + TILE) * 128,
            bytes_accessed=heads * span * 128 * 12,
            transcendentals=heads * span * (span + TILE),
        ),
    )(tiles_needed, slopes, firsts, queries, own, halo)


def own_kernel(
    inv_root, first, q_place, tiles_ref, slopes_ref, firsts_ref, q_ref, own_ref, earlier_ref,
    part_ref, value_win,
):
    span = q_ref.shape[0]
    heads = part_ref.shape[0]
    tiles = span // TILE
    wide = heads * 128
    for head in range(heads):
        value_win[head, 128:, :] = jnp.ones((16, span), jnp.bfloat16)
        value_win[head, :128, :] = own_ref[:, wide + head * 128 : wide + (head + 1) * 128].T
    firsts = firsts_ref[...]

    def one_tile(tile, _):
        row = pl.multiple_of(tile * TILE, TILE)
        needed = jnp.minimum(tiles_ref[tile], tile + 1)
        at = lax.broadcasted_iota(jnp.int32, (128, TILE), 1) + (span + row)
        begin_all = jnp.max(jnp.where(firsts <= at, firsts, 0), axis=0, keepdims=True)

        for count in range(1, tiles + 1):

            @pl.when(needed == count)
            def _():
                width = count * TILE
                base = pl.multiple_of((tile + 1 - count) * TILE, TILE)
                begin = begin_all - span - base
                offset = lax.broadcasted_iota(jnp.int32, (width, TILE), 0)
                distance = (offset - width).astype(jnp.float32)
                key_in = lax.broadcasted_iota(jnp.int32, (TILE, TILE), 0)
                query_in = lax.broadcasted_iota(jnp.int32, (TILE, TILE), 1)
                in_document = offset >= begin
                past = key_in <= query_in
                all_scores = []
                for head in range(heads):
                    all_scores.append(
                        lax.dot_general(
                            own_ref[pl.ds(base, width), head * 128 : (head + 1) * 128],
                            q_ref[pl.ds(row, TILE), pl.ds((q_place + head) * 128, 128)],
                            (((1,), (1,)), ((), ())),
                            preferred_element_type=jnp.float32,
                        )
                    )
                for head, scores in enumerate(all_scores):
                    slope = slopes_ref[first + head] * LOG2E
                    scores = scores * (inv_root * LOG2E) + slope * distance
                    scores = jnp.where(in_document, scores, NEG_FILL)
                    last = jnp.where(past, scores[width - TILE :], NEG_FILL)
                    if count > 1:
                        scores = jnp.concatenate([scores[: width - TILE], last], axis=0)
                    else:
                        scores = last
                    all_scores[head] = scores
                tops = [jnp.max(scores, axis=0, keepdims=True) for scores in all_scores]
                all_weights = [
                    jnp.exp2(scores - top).astype(jnp.bfloat16)
                    for scores, top in zip(all_scores, tops)
                ]
                for head, weights in enumerate(all_weights):
                    both = lax.dot_general(
                        value_win[head, :, pl.ds(base, width)],
                        weights,
                        (((1,), (0,)), ((), ())),
                        preferred_element_type=jnp.float32,
                    )
                    part_ref[head, :136, pl.ds(row, TILE)] = both[:136]
                    part_ref[head, 136:, pl.ds(row, TILE)] = jnp.broadcast_to(tops[head], (8, TILE))

        return 0

    lax.fori_loop(0, tiles, one_tile, 0)


def attend_own(tiles_needed, slopes, firsts, queries, own, earlier, first, heads, q_place):
    span = queries.shape[0]
    smem = pl.BlockSpec(memory_space=pltpu.SMEM)
    vmem = pl.BlockSpec(memory_space=pltpu.VMEM)
    return pl.pallas_call(
        functools.partial(own_kernel, 1.0 / math.sqrt(128), first, q_place),
        out_shape=jax.ShapeDtypeStruct((heads, 144, span), jnp.float32),
        in_specs=[smem, smem, vmem, vmem, vmem, pl.BlockSpec(memory_space=pl.ANY)],
        out_specs=vmem,
        scratch_shapes=[pltpu.VMEM((heads, 144, span), jnp.bfloat16)],
        compiler_params=pltpu.CompilerParams(vmem_limit_bytes=32 << 20),
        cost_estimate=pl.CostEstimate(
            flops=heads * 2 * span * (span + TILE) * 128,
            bytes_accessed=heads * span * 128 * 10,
            transcendentals=heads * span * (span + TILE) // 2,
        ),
    )(tiles_needed, slopes, firsts, queries, own, earlier)


def halo_kernel(
    inv_root, first, q_place, tiles_ref, slopes_ref, firsts_ref, q_ref, part_ref, halo_ref,
    out_ref, value_win,
):
    span = q_ref.shape[0]
    heads = part_ref.shape[0]
    tiles = span // TILE
    wide = heads * 128
    for head in range(heads):
        value_win[head, 128:, :] = jnp.ones((16, span), jnp.bfloat16)
        value_win[head, :128, :] = halo_ref[:, wide + head * 128 : wide + (head + 1) * 128].T
    firsts = firsts_ref[...]

    def one_tile(tile, _):
        row = pl.multiple_of(tile * TILE, TILE)
        needed = tiles_ref[tile] - (tile + 1)
        at = lax.broadcasted_iota(jnp.int32, (128, TILE), 1) + (span + row)
        begin_all = jnp.max(jnp.where(firsts <= at, firsts, 0), axis=0, keepdims=True)
        ahead = ((tile + 1) * TILE).astype(jnp.float32)

        def finish(head, sums, total):
            columns = slice(head * 128, (head + 1) * 128)
            result = sums * (1.0 / total)
            out_ref[pl.ds(row, TILE), columns] = result.T.astype(jnp.bfloat16)

        @pl.when(needed <= 0)
        def _():
            for head in range(heads):
                finish(
                    head,
                    part_ref[head, :128, pl.ds(row, TILE)],
                    part_ref[head, 128:129, pl.ds(row, TILE)],
                )

        for count in range(1, tiles + 1):

            @pl.when(needed == count)
            def _():
                width = count * TILE
                base = span - width
                offset = lax.broadcasted_iota(jnp.int32, (width, TILE), 0)
                distance = (offset - width).astype(jnp.float32) - ahead
                in_document = offset >= begin_all - base
                all_scores = []
                for head in range(heads):
                    all_scores.append(
                        lax.dot_general(
                            halo_ref[base:, head * 128 : (head + 1) * 128],
                            q_ref[pl.ds(row, TILE), pl.ds((q_place + head) * 128, 128)],
                            (((1,), (1,)), ((), ())),
                            preferred_element_type=jnp.float32,
                        )
                    )
                for head, scores in enumerate(all_scores):
                    slope = slopes_ref[first + head] * LOG2E
                    scores = scores * (inv_root * LOG2E) + slope * distance
                    all_scores[head] = jnp.where(in_document, scores, NEG_FILL)
                olds = [part_ref[head, 136:137, pl.ds(row, TILE)] for head in range(heads)]
                tops = [
                    jnp.maximum(old, jnp.max(scores, axis=0, keepdims=True))
                    for old, scores in zip(olds, all_scores)
                ]
                all_weights = [
                    jnp.exp2(scores - top).astype(jnp.bfloat16)
                    for scores, top in zip(all_scores, tops)
                ]
                for head, weights in enumerate(all_weights):
                    both = lax.dot_general(
                        value_win[head, :, base:],
                        weights,
                        (((1,), (0,)), ((), ())),
                        preferred_element_type=jnp.float32,
                    )
                    rescale = jnp.exp2(olds[head] - tops[head])
                    finish(
                        head,
                        both[:128] + rescale * part_ref[head, :128, pl.ds(row, TILE)],
                        both[128:129] + rescale * part_ref[head, 128:129, pl.ds(row, TILE)],
                    )

        return 0

    lax.fori_loop(0, tiles, one_tile, 0)


def attend_halo(tiles_needed, slopes, firsts, queries, part, halo, first, heads, q_place):
    span = queries.shape[0]
    smem = pl.BlockSpec(memory_space=pltpu.SMEM)
    vmem = pl.BlockSpec(memory_space=pltpu.VMEM)
    return pl.pallas_call(
        functools.partial(halo_kernel, 1.0 / math.sqrt(128), first, q_place),
        out_shape=jax.ShapeDtypeStruct((span, heads * 128), jnp.bfloat16),
        in_specs=[smem, smem, vmem, vmem, vmem, vmem],
        out_specs=vmem,
        scratch_shapes=[
            pltpu.VMEM((heads, 144, span), jnp.bfloat16),
        ],
        compiler_params=pltpu.CompilerParams(vmem_limit_bytes=32 << 20),
        cost_estimate=pl.CostEstimate(
            flops=heads * 2 * span * (span + TILE) * 128,
            bytes_accessed=heads * span * 128 * 10,
            transcendentals=heads * span * (span + TILE) // 2,
        ),
    )(tiles_needed, slopes, firsts, queries, part, halo)


def follow_kernel(value_ref, earlier_ref, out_ref):
    pass


def follow(value, earlier):
    anywhere = pl.BlockSpec(memory_space=pl.ANY)
    return pl.pallas_call(
        follow_kernel,
        out_shape=jax.ShapeDtypeStruct(value.shape, value.dtype),
        in_specs=[anywhere, anywhere],
        out_specs=anywhere,
        input_output_aliases={0: 0},
        compiler_params=pltpu.CompilerParams(vmem_limit_bytes=1 << 20),
    )(value, earlier)


def per_device(query_states, key_states, value_states, doc_lengths, slopes):
    rows = query_states.shape[0]
    outer, inner = lax.axis_size("outer"), lax.axis_size("inner")
    groups = 2 * inner
    supers = outer * inner // groups
    span = groups * rows
    count = slopes.shape[0] // groups
    me = lax.axis_index("outer") * inner + lax.axis_index("inner")
    super_index, member = me // groups, me % groups
    index_groups = [[s * groups + m for m in range(groups)] for s in range(supers)]
    onward = [(i, i + groups) for i in range((supers - 1) * groups)]

    def exchange(value):
        got = lax.all_to_all(value, AXES, 0, 0, axis_index_groups=index_groups)
        return got.reshape(span, value.shape[-1])

    own, halo, first_of, queries = [], [], [], {}
    next_kv, next_q = 0, 0
    for kv, q in IN_BATCHES:
        pieces = [(key_states, (next_kv, kv)), (value_states, (next_kv, kv))] * (kv > 0)
        pieces += [(query_states, (next_q, q))] * (q > 0)
        packed = pack([p[0] for p in pieces], tuple(p[1] for p in pieces), count, groups)
        got = exchange(packed)
        if kv:
            own.append(got)
            halo.append(lax.ppermute(got[:, : 2 * kv * 128], AXES, onward))
            first_of.append((next_kv, kv))
        for i in range(q):
            queries[next_q + i] = (got, 2 * kv + i)
        next_kv, next_q = next_kv + kv, next_q + q

    ids = jnp.arange(doc_lengths.shape[0])
    firsts = jnp.sum(jnp.where(ids[:, None] < ids[None, :], doc_lengths[:, None], 0), axis=0)
    firsts = firsts - (super_index - 1) * span
    tiles = span // TILE
    block = jnp.arange(tiles, dtype=jnp.int32)
    starts = jnp.max(jnp.where(firsts[None, :] <= (span + block * TILE)[:, None], firsts[None, :], 0), axis=1)
    needed = block + tiles + 1 - starts // TILE
    my_slopes = lax.dynamic_slice(slopes, (member * count,), (count,))

    outs = []
    for i, (first, heads) in enumerate(first_of):
        asked, q_place = queries[first]
        about = (needed, my_slopes, firsts[:, None], asked)
        if i == 0:
            done = attend(*about, own[i], halo[i], first, heads, q_place)
        else:
            part = attend_own(*about, own[i], own[i], first, heads, q_place)
            done = attend_halo(*about, part, halo[i], first, heads, q_place)
        sent = done.reshape(groups, rows, heads * 128)
        if outs:
            sent = follow(sent, outs[-1])
        outs.append(lax.all_to_all(sent, AXES, 0, 0, axis_index_groups=index_groups))
    return unpack(outs, count)


def solution(mesh):
    tokens = P(AXES, None)
    return jax.shard_map(
        per_device,
        mesh=mesh,
        in_specs=(tokens, tokens, tokens, P(), P()),
        out_specs=tokens,
        check_vma=False,
    )
```
